32 devices in a mesh: rep: 2 (over y), ep: 8 (over z, x), tp: 2 (over core).
Axes of the slice: x: 2, y: 2, z: 4, core: 2. Of those that a mesh axis runs over, the one named last changes fastest.
Arguments:
- tokens: bfloat16 [2048, 6144], P(('rep', 'ep'), 'tp'), parts along dimension 0, may hold values from -6 to 6
- expert_ids: int32 [2048, 4], P(('rep', 'ep')), parts along dimension 0, may hold values from 0 to 15, as said below
- gate_int: int32 [2048, 4], P(('rep', 'ep')), parts along dimension 0, may hold values from 1 to 64
- w_gate: bfloat16 [8, 6144, 2688], P('ep', 'tp'), may hold values from -0.078125 to 0.078125
- w_up: bfloat16 [8, 6144, 2688], P('ep', 'tp'), may hold values from -0.078125 to 0.078125
- w_down: bfloat16 [8, 2688, 6144], P('ep', None, 'tp'), may hold values from -0.078125 to 0.078125
Outputs:
- combined: bfloat16 [2048, 6144], P(('rep', 'ep'), 'tp'), parts along dimension 0
The draws below stay inside these ranges and needn't reach their ends.
There are 2 independent parts, one for each index of `rep`. The reference program is written for one: setup_inputs(seed, part) draws one part's arguments, and reference() takes and returns one part's arrays. A program takes and returns all parts, laid end to end along the dimension named above; an argument that names none is the same for every part. Nothing has to cross between parts.
Inputs may be any that keep to these rules, and one draw needn't show every extreme that they name: `expert_ids`: each row names 4 different experts. In the 128 rows of one index of ep, one held expert (the same in every block of a draw, drawn from the seed) is named by exactly 32 rows, and every other held expert by 1 to 16 rows.
All inputs are finite; a program needn't handle non-finite values.
Results may differ from the reference program's by a relative error of at most 0.0058.
Values may be sent and summed in bfloat16 or wider, within the bound.
A program may use at most 128 MiB of HBM per device.

```python
import jax
import jax.numpy as jnp

D = 6144
FF = 5376
EXPERTS = 16
TOPK = 4
HELD = 4
TOK_DEV = 128
CAP = 32
HIDS = 2688
SLICES = 8
TOKENS = 1024
N_EP = 8


def draw_expert_ids(key, part):
    key = jax.random.fold_in(key, 17)
    subkeys = jax.random.split(key, 5)
    block_count = TOKENS // TOK_DEV
    hot_expert = jax.random.randint(subkeys[0], (), 0, HELD)
    light_counts = jax.random.randint(subkeys[1], (block_count, HELD), 1, CAP // 2 + 1)
    row_counts = jnp.where(jnp.arange(HELD, dtype=jnp.int32)[None, :] == hot_expert, CAP, light_counts)
    row_scores = jax.random.randint(subkeys[2], (block_count, HELD, TOK_DEV), 0, 2 ** 20) * TOK_DEV + jnp.arange(TOK_DEV, dtype=jnp.int32)[None, None, :]
    row_ranks = jnp.argsort(jnp.argsort(row_scores, axis=2), axis=2)
    is_member = row_ranks < row_counts[:, :, None]
    is_member = jnp.transpose(is_member, (0, 2, 1)).reshape(TOKENS, HELD)
    outside_count = EXPERTS - HELD
    other_scores = jax.random.randint(subkeys[3], (TOKENS, outside_count), 0, 2 ** 20) * outside_count + jnp.arange(outside_count, dtype=jnp.int32)[None, :]
    other_ids = jnp.argsort(other_scores, axis=1)[:, :TOPK].astype(jnp.int32) + HELD
    candidates = jnp.concatenate([jnp.broadcast_to(jnp.arange(HELD, dtype=jnp.int32)[None, :], (TOKENS, HELD)), other_ids], axis=1)
    held_keys = jnp.where(is_member, 0, 2 * TOPK + 2).astype(jnp.int32)
    other_keys = jnp.broadcast_to(1 + jnp.arange(TOPK, dtype=jnp.int32)[None, :], (TOKENS, TOPK))
    picked_cols = jnp.argsort(jnp.concatenate([held_keys, other_keys], axis=1), axis=1, stable=True)[:, :TOPK]
    chosen_ids = jnp.take_along_axis(candidates, picked_cols, axis=1)
    mix_scores = jax.random.randint(subkeys[4], (TOKENS, TOPK), 0, 2 ** 20) * TOPK + jnp.arange(TOPK, dtype=jnp.int32)[None, :]
    return jnp.take_along_axis(chosen_ids, jnp.argsort(mix_scores, axis=1), axis=1).astype(jnp.int32)


def touch_ends(values, rng, least, largest):
    spot = [jax.random.randint(jax.random.fold_in(rng, axis), (), 0, length) for axis, length in enumerate(values.shape)]
    main_axis = values.shape.index(max(values.shape))
    neighbour = spot[:main_axis] + [(spot[main_axis] + 1) % values.shape[main_axis]] + spot[main_axis + 1:]
    return values.at[tuple(spot)].set(least).at[tuple(neighbour)].set(largest)


def block_scale(key, shape, cuts, low, high):
    gain = 1.0
    for axis_at, shards_of in cuts:
        heights = jax.random.uniform(jax.random.fold_in(jax.random.fold_in(key, 6), axis_at), (shards_of,), jnp.float32, low / len(cuts), high / len(cuts))
        gain = gain * jnp.repeat(jnp.exp(heights), shape[axis_at] // shards_of).reshape((-1,) + (1,) * (len(shape) - 1 - axis_at))
    return gain


def centred(own_key, dims, scale, reach, pieces=(), held_as=jnp.bfloat16):
    result = jax.random.normal(own_key, dims, jnp.float32) * scale
    if len(pieces) > 0:
        result = block_scale(own_key, dims, pieces, -0.22, 0.18) * result
    return jnp.clip(result, min=-reach, max=reach).astype(held_as)


def setup_inputs(seed: int = 0, part: int = 0) -> dict:
    key_list = jax.random.split(jax.random.key(seed), 7)
    own_keys = jax.random.split(jax.random.fold_in(key_list[6], part), 7)
    tokens = centred(own_keys[0], (TOKENS, D), 1.0, 6.0, ((0, 8), (1, 2)))
    expert_ids = draw_expert_ids(jax.random.fold_in(jax.random.fold_in(key_list[6], part), 71), part)
    gate_int = touch_ends(jax.random.randint(own_keys[2], (TOKENS, TOPK), 1, 65), jax.random.fold_in(own_keys[2], 1), 1, 64).astype(jnp.int32)
    w_gate = centred(key_list[3], (SLICES, D, HIDS), D ** -0.5, 0.078125, ((0, 8), (1, 2)))
    w_up = centred(key_list[4], (SLICES, D, HIDS), D ** -0.5, 0.078125, ((0, 8), (1, 2)))
    w_down = centred(key_list[5], (SLICES, HIDS, D), FF ** -0.5, 0.078125, ((0, 8), (2, 2)))
    return dict(tokens=tokens, expert_ids=expert_ids, gate_int=gate_int, w_gate=w_gate, w_up=w_up, w_down=w_down)


def reference(tokens, expert_ids, gate_int, w_gate, w_up, w_down):
    members = N_EP // HELD
    token_count = tokens.shape[0]
    block_count = token_count // TOK_DEV
    combined = jnp.zeros(tokens.shape, jnp.float32)
    for expert in range(HELD):
        named = expert_ids == expert
        weighting = jnp.sum(jnp.where(named, gate_int.astype(jnp.float32) / 64.0, jnp.float32(0.0)), axis=1)
        chosen = jnp.any(named, axis=1).astype(jnp.int32).reshape(block_count, TOK_DEV)
        ordering = jnp.argsort(1 - chosen, axis=1, stable=True)[:, :CAP].astype(jnp.int32)
        offsets = (jnp.arange(block_count, dtype=jnp.int32) * TOK_DEV)[:, None]
        picked = (ordering + offsets).reshape(-1).astype(jnp.int32)
        rows_in = tokens[picked]
        expert_sum = jnp.zeros((picked.shape[0], tokens.shape[1]), jnp.float32)
        for member in range(members):
            slice_id = expert * members + member
            gate_part = jnp.dot(rows_in, w_gate[slice_id], preferred_element_type=jnp.float32)
            up_part = jnp.dot(rows_in, w_up[slice_id], preferred_element_type=jnp.float32)
            hidden = (jax.nn.silu(gate_part) * up_part).astype(jnp.bfloat16)
            partial_value = jnp.dot(hidden, w_down[slice_id], preferred_element_type=jnp.float32).astype(jnp.bfloat16)
            expert_sum = expert_sum + partial_value.astype(jnp.float32)
        combined = combined.at[picked].add(weighting[picked][:, None] * expert_sum)
    return combined.astype(jnp.bfloat16)
```

```python
import functools

import jax
import jax.numpy as jnp
from jax import lax
from jax.experimental import pallas as pl
from jax.experimental.pallas import tpu as pltpu
from jax.sharding import PartitionSpec as P

HELD = 4
CAP = 32
MEMBERS = 2
K_CHUNKS = 4
OUT_COLS = 512
HID_COLS = 512
DOWN_SLOTS = 3


def remote(src, dst, send_sem, recv_sem, axis, index):
    return pltpu.make_async_remote_copy(
        src_ref=src,
        dst_ref=dst,
        send_sem=send_sem,
        recv_sem=recv_sem,
        device_id={axis: index},
        device_id_type=pl.DeviceIdType.MESH,
    )


def fused_kernel(
    ids_ref, gint_ref, tok_hbm, wg_hbm, wu_hbm, wd_hbm, out_ref,
    tok, wg, wu, wd, send, recv, acc_g, acc_u, gu_send, gu_recv, hid,
    part, part_in, own, total, ret,
    tok_sem, wg_sem, wu_sem, wd_sem,
    z_send, z_recv, x_send, x_recv, gu_ss, gu_rs, hid_ss, hid_rs,
    px_send, px_recv, rz_send, rz_recv,
):
    rows, depth = tok.shape
    hidden = wg.shape[1]
    out_cols = wd.shape[2]
    out_chunks = part.shape[0]
    kw = depth // K_CHUNKS
    half = HELD * CAP
    me = lax.axis_index("ep")
    mine = lax.div(me, MEMBERS)
    x = lax.rem(me, MEMBERS)
    t = lax.axis_index("tp")
    x_peer = mine * MEMBERS + 1 - x
    t_peer = 1 - t
    my_row = pl.multiple_of(t * half, half)
    peer_row = pl.multiple_of(t_peer * half, half)
    full_tiles = hidden // HID_COLS
    tail = hidden % HID_COLS

    def z_to(d):
        return lax.rem(mine + d, HELD)

    def z_from(d):
        return lax.rem(mine + HELD - d, HELD)

    def over_tiles(body):
        def step(n, carry):
            body(n, pl.ds(pl.multiple_of(n * HID_COLS, HID_COLS), HID_COLS))
            return carry

        lax.fori_loop(0, full_tiles, step, 0)
        if tail:
            body(full_tiles, pl.ds(full_tiles * HID_COLS, tail))

    tok_copy = pltpu.make_async_copy(tok_hbm, tok, tok_sem)
    tok_copy.start()

    def weight_copies(k):
        band = pl.ds(k * kw, kw)
        return (
            pltpu.make_async_copy(wg_hbm.at[0, band], wg.at[band], wg_sem.at[k]),
            pltpu.make_async_copy(wu_hbm.at[0, band], wu.at[band], wu_sem.at[k]),
        )

    def down_copy(c):
        return pltpu.make_async_copy(
            wd_hbm.at[0, :, pl.ds(c * out_cols, out_cols)],
            wd.at[c % DOWN_SLOTS],
            wd_sem.at[c % DOWN_SLOTS],
        )

    for k in range(K_CHUNKS):
        for copy in weight_copies(k):
            copy.start()
    for c in range(min(DOWN_SLOTS, out_chunks)):
        down_copy(c).start()

    barrier = pltpu.get_barrier_semaphore()
    for d in range(1, HELD):
        pl.semaphore_signal(
            barrier, inc=1, device_id={"ep": z_to(d) * MEMBERS + x},
            device_id_type=pl.DeviceIdType.MESH,
        )
    pl.semaphore_signal(
        barrier, inc=1, device_id={"ep": x_peer}, device_id_type=pl.DeviceIdType.MESH
    )
    pl.semaphore_signal(
        barrier, inc=1, device_id={"tp": t_peer}, device_id_type=pl.DeviceIdType.MESH
    )

    lane = lax.broadcasted_iota(jnp.int32, (rows, half), 1)
    lane_expert = lax.div(lane, CAP)
    lane_slot = lax.rem(lane, CAP).astype(jnp.float32)
    chosen = jnp.zeros((rows, half), jnp.float32)
    weight = jnp.zeros((rows, half), jnp.float32)
    for j in range(ids_ref.shape[1]):
        hit = ids_ref[:, j : j + 1] == lane_expert
        chosen = chosen + jnp.where(hit, 1.0, 0.0)
        weight = weight + jnp.where(hit, gint_ref[:, j : j + 1].astype(jnp.float32) / 64.0, 0.0)
    lower = (
        lax.broadcasted_iota(jnp.int32, (rows, rows), 0)
        >= lax.broadcasted_iota(jnp.int32, (rows, rows), 1)
    )
    rank = jnp.dot(
        jnp.where(lower, 1.0, 0.0).astype(jnp.bfloat16),
        chosen.astype(jnp.bfloat16),
        preferred_element_type=jnp.float32,
    )
    placed = jnp.where(rank == lane_slot + 1.0, chosen, 0.0)
    weighted = (placed * weight).astype(jnp.bfloat16)
    placed = placed.astype(jnp.bfloat16)

    pl.semaphore_wait(barrier, HELD + 1)
    tok_copy.wait()

    def z_copy(k, d):
        return remote(
            send.at[k, z_to(d)], recv.at[k, 0, mine], z_send.at[k, d - 1],
            z_recv.at[k, d - 1], "ep", z_to(d) * MEMBERS + x,
        )

    def x_copy(k, d):
        block = z_from(d)
        return remote(
            recv.at[k, 0, block], recv.at[k, 1, block], x_send.at[k, d],
            x_recv.at[k, d], "ep", x_peer,
        )

    for k in range(K_CHUNKS):
        packed = lax.dot_general(
            placed, tok[:, k * kw : (k + 1) * kw], (((0,), (0,)), ((), ())),
            preferred_element_type=jnp.float32,
        ).astype(jnp.bfloat16)
        send[k] = packed.reshape(HELD, CAP, kw)
        for d in (2, 1, 3):
            z_copy(k, d).start()
        recv[k, 0, mine] = send[k, mine]
        x_copy(k, 0).start()

    def forward(k):
        for d in (1, 3, 2):
            z_copy(k, d).wait_recv()
            x_copy(k, d).start()

    def project(k):
        for copy in weight_copies(k):
            copy.wait()
        for d in range(HELD):
            x_copy(k, d).wait_recv()
        band = pl.ds(k * kw, kw)

        def tile(n, cols):
            lhs = recv[k].reshape(MEMBERS * half, kw)
            for w, acc in ((wg, acc_g), (wu, acc_u)):
                value = jnp.dot(lhs, w[band, cols], preferred_element_type=jnp.float32)
                if k > 0:
                    value = value + acc[:, cols]
                acc[:, cols] = value
            if k == K_CHUNKS - 1:
                for i, acc in enumerate((acc_g, acc_u)):
                    gu_send[i, :, cols] = acc[pl.ds(peer_row, half), cols].astype(jnp.bfloat16)
                gu_copy(n, cols).start()

        over_tiles(tile)

    def gu_copy(n, cols):
        return remote(
            gu_send.at[:, :, cols], gu_recv.at[:, :, cols], gu_ss.at[n], gu_rs.at[n], "tp", t_peer
        )

    def hid_copy(n, cols):
        span = hid.at[pl.ds(my_row, half), cols]
        return remote(span, span, hid_ss.at[n], hid_rs.at[n], "tp", t_peer)

    forward(0)
    for k in range(1, K_CHUNKS):
        forward(k)
        project(k - 1)
    project(K_CHUNKS - 1)

    def activate(n, cols):
        gu_copy(n, cols).wait_recv()
        gate = acc_g[pl.ds(my_row, half), cols] + gu_recv[0, :, cols].astype(jnp.float32)
        up = acc_u[pl.ds(my_row, half), cols] + gu_recv[1, :, cols].astype(jnp.float32)
        hid[pl.ds(my_row, half), cols] = (jax.nn.silu(gate) * up).astype(jnp.bfloat16)
        hid_copy(n, cols).start()

    over_tiles(activate)
    over_tiles(lambda n, cols: hid_copy(n, cols).wait_recv())

    def part_copy(c):
        return remote(part.at[c], part_in.at[c], px_send.at[c], px_recv.at[c], "ep", x_peer)

    def ret_copy(c, d):
        return remote(
            total.at[c, z_to(d)], ret.at[c, mine], rz_send.at[c, d - 1], rz_recv.at[c, d - 1],
            "ep", z_to(d) * MEMBERS + x,
        )

    for c in range(out_chunks):
        down_copy(c).wait()
        value = jnp.dot(
            hid[...], wd[c % DOWN_SLOTS], preferred_element_type=jnp.float32
        ).astype(jnp.bfloat16)
        part[c] = value[half:]
        part_copy(c).start()
        own[c] = value[:half]
        if c + DOWN_SLOTS < out_chunks:
            down_copy(c + DOWN_SLOTS).start()

    for c in range(out_chunks):
        part_copy(c).wait_recv()
        value = (own[c].astype(jnp.float32) + part_in[c].astype(jnp.float32)).astype(jnp.bfloat16)
        total[c] = value.reshape(HELD, CAP, out_cols)
        for d in (2, 1, 3):
            ret_copy(c, d).start()
        ret[c, mine] = total[c, mine]

    for c in range(out_chunks):
        for d in range(1, HELD):
            ret_copy(c, d).wait_recv()
        out_ref[:, c * out_cols : (c + 1) * out_cols] = jnp.dot(
            weighted, ret[c].reshape(half, out_cols), preferred_element_type=jnp.float32
        ).astype(jnp.bfloat16)

    for k in range(K_CHUNKS):
        for d in range(HELD):
            x_copy(k, d).wait_send()
            if d > 0:
                z_copy(k, d).wait_send()
    over_tiles(lambda n, cols: gu_copy(n, cols).wait_send())
    over_tiles(lambda n, cols: hid_copy(n, cols).wait_send())
    for c in range(out_chunks):
        part_copy(c).wait_send()
        for d in range(1, HELD):
            ret_copy(c, d).wait_send()


def fused_shards(tokens, expert_ids, gate_int, w_gate, w_up, w_down):
    rows, depth = tokens.shape
    hidden = w_gate.shape[2]
    columns = w_down.shape[2]
    out_chunks = columns // OUT_COLS
    half = HELD * CAP
    kw = depth // K_CHUNKS
    tiles = pl.cdiv(hidden, HID_COLS)
    bf16, f32 = jnp.bfloat16, jnp.float32
    dma = pltpu.SemaphoreType.DMA
    return pl.pallas_call(
        fused_kernel,
        out_shape=jax.ShapeDtypeStruct((rows, columns), bf16),
        in_specs=[pl.BlockSpec(memory_space=pltpu.VMEM)] * 2
        + [pl.BlockSpec(memory_space=pl.ANY)] * 4,
        out_specs=pl.BlockSpec(memory_space=pltpu.VMEM),
        scratch_shapes=[
            pltpu.VMEM((rows, depth), bf16),
            pltpu.VMEM((depth, hidden), bf16),
            pltpu.VMEM((depth, hidden), bf16),
            pltpu.VMEM((DOWN_SLOTS, hidden, OUT_COLS), bf16),
            pltpu.VMEM((K_CHUNKS, HELD, CAP, kw), bf16),
            pltpu.VMEM((K_CHUNKS, MEMBERS, HELD, CAP, kw), bf16),
            pltpu.VMEM((MEMBERS * half, hidden), f32),
            pltpu.VMEM((MEMBERS * half, hidden), f32),
            pltpu.VMEM((2, half, hidden), bf16),
            pltpu.VMEM((2, half, hidden), bf16),
            pltpu.VMEM((MEMBERS * half, hidden), bf16),
            pltpu.VMEM((out_chunks, half, OUT_COLS), bf16),
            pltpu.VMEM((out_chunks, half, OUT_COLS), bf16),
            pltpu.VMEM((out_chunks, half, OUT_COLS), bf16),
            pltpu.VMEM((out_chunks, HELD, CAP, OUT_COLS), bf16),
            pltpu.VMEM((out_chunks, HELD, CAP, OUT_COLS), bf16),
            dma, dma((K_CHUNKS,)), dma((K_CHUNKS,)), dma((DOWN_SLOTS,)),
            dma((K_CHUNKS, HELD - 1)), dma((K_CHUNKS, HELD - 1)),
            dma((K_CHUNKS, HELD)), dma((K_CHUNKS, HELD)),
            dma((tiles,)), dma((tiles,)), dma((tiles,)), dma((tiles,)),
            dma((out_chunks,)), dma((out_chunks,)),
            dma((out_chunks, HELD - 1)), dma((out_chunks, HELD - 1)),
        ],
        compiler_params=pltpu.CompilerParams(
            collective_id=0, has_side_effects=True, vmem_limit_bytes=64000000
        ),
        cost_estimate=pl.CostEstimate(
            flops=12 * half * depth * hidden, bytes_accessed=6 * depth * hidden, transcendentals=0
        ),
    )(expert_ids, gate_int, tokens, w_gate, w_up, w_down)


def silu_product(gate_up):
    return (jax.nn.silu(gate_up[:, 0]) * gate_up[:, 1]).astype(jnp.bfloat16)


def expert_rows(received, w_gate, w_up, w_down):
    columns = received.shape[-1]
    leading = received.shape[:-1]
    flattened = received.reshape(-1, columns)
    gate_part = jnp.dot(flattened, w_gate[0], preferred_element_type=jnp.float32)
    up_part = jnp.dot(flattened, w_up[0], preferred_element_type=jnp.float32)
    gate_up = jnp.stack([gate_part, up_part], axis=1)
    summed_half = lax.psum_scatter(gate_up, "tp", scatter_dimension=2, tiled=True)
    hidden = lax.all_gather(silu_product(summed_half), "tp", axis=1, tiled=True)
    partial_value = jnp.dot(hidden, w_down[0], preferred_element_type=jnp.float32).astype(
        jnp.bfloat16
    )
    return partial_value.reshape(leading + (partial_value.shape[-1],))


def send_back(partial_value):
    return lax.all_to_all(partial_value, "ep", split_axis=0, concat_axis=0, tiled=True)


def fits(tokens, w_gate, w_down):
    depth, hidden = w_gate.shape[1:]
    return (
        lax.axis_size("ep") == HELD * MEMBERS
        and lax.axis_size("tp") == 2
        and tokens.shape[0] == HELD * CAP
        and depth % (128 * K_CHUNKS) == 0
        and hidden % 128 == 0
        and w_down.shape[2] % OUT_COLS == 0
    )


def shards(tokens, expert_ids, gate_int, w_gate, w_up, w_down):
    if fits(tokens, w_gate, w_down):
        return fused_shards(tokens, expert_ids, gate_int, w_gate, w_up, w_down)
    row_count = tokens.shape[0]
    experts = lax.broadcasted_iota(jnp.int32, (HELD, 1, 1), 0)
    named = expert_ids[None, :, :] == experts
    weighting = jnp.sum(
        jnp.where(named, gate_int[None, :, :].astype(jnp.float32) / 64.0, jnp.float32(0.0)), axis=2
    )
    chosen = jnp.any(named, axis=2).astype(jnp.int32)
    slot_of = jnp.cumsum(chosen, axis=1) - 1
    slot_ids = lax.broadcasted_iota(jnp.int32, (HELD, CAP, row_count), 1)
    placed = (chosen[:, None, :] == 1) & (slot_of[:, None, :] == slot_ids)
    outgoing = jnp.einsum(
        "ecr,rd->ecd", placed.astype(jnp.bfloat16), tokens, preferred_element_type=jnp.float32
    ).astype(jnp.bfloat16)
    members = lax.axis_size("ep") // HELD
    outgoing = jnp.repeat(outgoing, members, axis=0)
    received = lax.all_to_all(outgoing, "ep", split_axis=0, concat_axis=0, tiled=True)
    returned = send_back(expert_rows(received, w_gate, w_up, w_down))
    columns = returned.shape[-1]
    summed = jnp.sum(returned.reshape(HELD, members, CAP, columns).astype(jnp.float32), axis=1)
    weighted = placed.astype(jnp.float32) * weighting[:, None, :]
    combined = jnp.einsum("ecr,ecd->rd", weighted, summed, precision=lax.Precision.HIGHEST)
    return combined.astype(jnp.bfloat16)


def solution(mesh):
    return jax.shard_map(
        shards,
        mesh=mesh,
        in_specs=(
            P(("rep", "ep"), "tp"),
            P(("rep", "ep"), None),
            P(("rep", "ep"), None),
            P("ep", "tp", None),
            P("ep", "tp", None),
            P("ep", None, "tp"),
        ),
        out_specs=P(("rep", "ep"), "tp"),
        check_vma=False,
    )
```

```python
import functools

import jax
import jax.numpy as jnp
from jax import lax
from jax.experimental import pallas as pl
from jax.experimental.pallas import tpu as pltpu
from jax.sharding import PartitionSpec as P

HELD = 4
CAP = 32
MEMBERS = 2
K_CHUNKS = 3
OUT_COLS = 768
HID_COLS = 512
DOWN_SLOTS = 2


def remote(src, dst, send_sem, recv_sem, axis, index):
    return pltpu.make_async_remote_copy(
        src_ref=src,
        dst_ref=dst,
        send_sem=send_sem,
        recv_sem=recv_sem,
        device_id={axis: index},
        device_id_type=pl.DeviceIdType.MESH,
    )


def fused_kernel(
    ids_ref, gint_ref, tok_hbm, wg_hbm, wu_hbm, wd_hbm, out_ref,
    tok, wg, wu, wd, send, recv, acc_g, acc_u, gu_send, gu_recv, hid,
    part, part_in, own, total, ret,
    tok_sem, wg_sem, wu_sem, wd_sem,
    z_send, z_recv, x_send, x_recv, gu_ss, gu_rs, hid_ss, hid_rs,
    px_send, px_recv, rz_send, rz_recv,
):
    rows, depth = tok.shape
    hidden = wg.shape[1]
    out_cols = wd.shape[2]
    out_chunks = part.shape[0]
    kw = depth // K_CHUNKS
    half = HELD * CAP
    me = lax.axis_index("ep")
    mine = lax.div(me, MEMBERS)
    x = lax.rem(me, MEMBERS)
    t = lax.axis_index("tp")
    x_peer = mine * MEMBERS + 1 - x
    t_peer = 1 - t
    my_row = pl.multiple_of(t * half, half)
    peer_row = pl.multiple_of(t_peer * half, half)
    full_tiles = hidden // HID_COLS
    tail = hidden % HID_COLS

    def z_to(d):
        return lax.rem(mine + d, HELD)

    def z_from(d):
        return lax.rem(mine + HELD - d, HELD)

    def over_tiles(body):
        def step(n, carry):
            body(n, pl.ds(pl.multiple_of(n * HID_COLS, HID_COLS), HID_COLS))
            return carry

        lax.fori_loop(0, full_tiles, step, 0)
        if tail:
            body(full_tiles, pl.ds(full_tiles * HID_COLS, tail))

    tok_copy = pltpu.make_async_copy(tok_hbm, tok, tok_sem)
    tok_copy.start()

    def weight_copies(k):
        band = pl.ds(k * kw, kw)
        return (
            pltpu.make_async_copy(wg_hbm.at[0, band], wg.at[band], wg_sem.at[k]),
            pltpu.make_async_copy(wu_hbm.at[0, band], wu.at[band], wu_sem.at[k]),
        )

    def down_copy(c):
        return pltpu.make_async_copy(
            wd_hbm.at[0, :, pl.ds(c * out_cols, out_cols)],
            wd.at[c % DOWN_SLOTS],
            wd_sem.at[c % DOWN_SLOTS],
        )

    for k in range(K_CHUNKS):
        for copy in weight_copies(k):
            copy.start()
    for c in range(min(DOWN_SLOTS, out_chunks)):
        down_copy(c).start()

    barrier = pltpu.get_barrier_semaphore()
    for d in range(1, HELD):
        pl.semaphore_signal(
            barrier, inc=1, device_id={"ep": z_to(d) * MEMBERS + x},
            device_id_type=pl.DeviceIdType.MESH,
        )
    pl.semaphore_signal(
        barrier, inc=1, device_id={"ep": x_peer}, device_id_type=pl.DeviceIdType.MESH
    )
    pl.semaphore_signal(
        barrier, inc=1, device_id={"tp": t_peer}, device_id_type=pl.DeviceIdType.MESH
    )

    spot = lax.broadcasted_iota(jnp.int32, (half, rows), 0)
    spot_expert = lax.div(spot, CAP)
    spot_slot = lax.rem(spot, CAP).astype(jnp.float32)
    chosen = jnp.zeros((half, rows), jnp.float32)
    weight = jnp.zeros((half, rows), jnp.float32)
    for j in range(ids_ref.shape[0]):
        hit = ids_ref[j : j + 1] == spot_expert
        chosen = chosen + jnp.where(hit, 1.0, 0.0)
        weight = weight + jnp.where(hit, gint_ref[j : j + 1].astype(jnp.float32) / 64.0, 0.0)
    upper = (
        lax.broadcasted_iota(jnp.int32, (rows, rows), 0)
        <= lax.broadcasted_iota(jnp.int32, (rows, rows), 1)
    )
    rank = jnp.dot(
        chosen.astype(jnp.bfloat16),
        jnp.where(upper, 1.0, 0.0).astype(jnp.bfloat16),
        preferred_element_type=jnp.float32,
    )
    placed = jnp.where(rank == spot_slot + 1.0, chosen, 0.0)
    weighted = jnp.transpose(placed * weight).astype(jnp.bfloat16)
    placed = placed.astype(jnp.bfloat16)

    pl.semaphore_wait(barrier, HELD + 1)
    tok_copy.wait()

    def z_copy(k, d):
        return remote(
            send.at[k, z_to(d)], recv.at[k, 0, mine], z_send.at[k, d - 1],
            z_recv.at[k, d - 1], "ep", z_to(d) * MEMBERS + x,
        )

    def x_copy(k, d):
        block = z_from(d)
        return remote(
            recv.at[k, 0, block], recv.at[k, 1, block], x_send.at[k, d],
            x_recv.at[k, d], "ep", x_peer,
        )

    for k in range(K_CHUNKS):
        packed = jnp.dot(
            placed, tok[:, k * kw : (k + 1) * kw], preferred_element_type=jnp.float32
        ).astype(jnp.bfloat16)
        send[k] = packed.reshape(HELD, CAP, kw)
        for d in (2, 1, 3):
            z_copy(k, d).start()
        recv[k, 0, mine] = send[k, mine]
        x_copy(k, 0).start()

    def forward(k):
        for d in (1, 3, 2):
            z_copy(k, d).wait_recv()
            x_copy(k, d).start()

    def project(k):
        for copy in weight_copies(k):
            copy.wait()
        for d in range(HELD):
            x_copy(k, d).wait_recv()
        band = pl.ds(k * kw, kw)

        def tile(n, cols):
            lhs = recv[k].reshape(MEMBERS * half, kw)
            for w, acc in ((wg, acc_g), (wu, acc_u)):
                value = jnp.dot(lhs, w[band, cols], preferred_element_type=jnp.float32)
                if k > 0:
                    value = value + acc[:, cols]
                acc[:, cols] = value
            if k == K_CHUNKS - 1:
                for i, acc in enumerate((acc_g, acc_u)):
                    gu_send[i, :, cols] = acc[pl.ds(peer_row, half), cols].astype(jnp.bfloat16)
                gu_copy(n, cols).start()

        over_tiles(tile)

    def gu_copy(n, cols):
        return remote(
            gu_send.at[:, :, cols], gu_recv.at[:, :, cols], gu_ss.at[n], gu_rs.at[n], "tp", t_peer
        )

    def hid_copy(n, cols):
        span = hid.at[pl.ds(my_row, half), cols]
        return remote(span, span, hid_ss.at[n], hid_rs.at[n], "tp", t_peer)

    forward(0)
    for k in range(1, K_CHUNKS):
        forward(k)
        project(k - 1)
    project(K_CHUNKS - 1)

    def activate(n, cols):
        gu_copy(n, cols).wait_recv()
        gate = acc_g[pl.ds(my_row, half), cols] + gu_recv[0, :, cols].astype(jnp.float32)
        up = acc_u[pl.ds(my_row, half), cols] + gu_recv[1, :, cols].astype(jnp.float32)
        hid[pl.ds(my_row, half), cols] = (jax.nn.silu(gate) * up).astype(jnp.bfloat16)
        hid_copy(n, cols).start()

    over_tiles(activate)
    over_tiles(lambda n, cols: hid_copy(n, cols).wait_recv())

    def part_copy(c):
        return remote(part.at[c], part_in.at[c], px_send.at[c], px_recv.at[c], "ep", x_peer)

    def ret_copy(c, d):
        return remote(
            total.at[c, z_to(d)], ret.at[c, mine], rz_send.at[c, d - 1], rz_recv.at[c, d - 1],
            "ep", z_to(d) * MEMBERS + x,
        )

    for c in range(out_chunks):
        down_copy(c).wait()
        value = jnp.dot(
            hid[...], wd[c % DOWN_SLOTS], preferred_element_type=jnp.float32
        ).astype(jnp.bfloat16)
        part[c] = value[half:]
        part_copy(c).start()
        own[c] = value[:half]
        if c + DOWN_SLOTS < out_chunks:
            down_copy(c + DOWN_SLOTS).start()

    for c in range(out_chunks):
        part_copy(c).wait_recv()
        value = (own[c].astype(jnp.float32) + part_in[c].astype(jnp.float32)).astype(jnp.bfloat16)
        total[c] = value.reshape(HELD, CAP, out_cols)
        for d in (2, 1, 3):
            ret_copy(c, d).start()
        ret[c, mine] = total[c, mine]

    for c in range(out_chunks):
        for d in range(1, HELD):
            ret_copy(c, d).wait_recv()
        out_ref[:, c * out_cols : (c + 1) * out_cols] = jnp.dot(
            weighted, ret[c].reshape(half, out_cols), preferred_element_type=jnp.float32
        ).astype(jnp.bfloat16)

    for k in range(K_CHUNKS):
        for d in range(HELD):
            x_copy(k, d).wait_send()
            if d > 0:
                z_copy(k, d).wait_send()
    over_tiles(lambda n, cols: gu_copy(n, cols).wait_send())
    over_tiles(lambda n, cols: hid_copy(n, cols).wait_send())
    for c in range(out_chunks):
        part_copy(c).wait_send()
        for d in range(1, HELD):
            ret_copy(c, d).wait_send()


def fused_shards(tokens, expert_ids, gate_int, w_gate, w_up, w_down):
    rows, depth = tokens.shape
    hidden = w_gate.shape[2]
    columns = w_down.shape[2]
    out_chunks = columns // OUT_COLS
    half = HELD * CAP
    kw = depth // K_CHUNKS
    tiles = pl.cdiv(hidden, HID_COLS)
    bf16, f32 = jnp.bfloat16, jnp.float32
    dma = pltpu.SemaphoreType.DMA
    return pl.pallas_call(
        fused_kernel,
        out_shape=jax.ShapeDtypeStruct((rows, columns), bf16),
        in_specs=[pl.BlockSpec(memory_space=pltpu.VMEM)] * 2
        + [pl.BlockSpec(memory_space=pl.ANY)] * 4,
        out_specs=pl.BlockSpec(memory_space=pltpu.VMEM),
        scratch_shapes=[
            pltpu.VMEM((rows, depth), bf16),
            pltpu.VMEM((depth, hidden), bf16),
            pltpu.VMEM((depth, hidden), bf16),
            pltpu.VMEM((DOWN_SLOTS, hidden, OUT_COLS), bf16),
            pltpu.VMEM((K_CHUNKS, HELD, CAP, kw), bf16),
            pltpu.VMEM((K_CHUNKS, MEMBERS, HELD, CAP, kw), bf16),
            pltpu.VMEM((MEMBERS * half, hidden), f32),
            pltpu.VMEM((MEMBERS * half, hidden), f32),
            pltpu.VMEM((2, half, hidden), bf16),
            pltpu.VMEM((2, half, hidden), bf16),
            pltpu.VMEM((MEMBERS * half, hidden), bf16),
            pltpu.VMEM((out_chunks, half, OUT_COLS), bf16),
            pltpu.VMEM((out_chunks, half, OUT_COLS), bf16),
            pltpu.VMEM((out_chunks, half, OUT_COLS), bf16),
            pltpu.VMEM((out_chunks, HELD, CAP, OUT_COLS), bf16),
            pltpu.VMEM((out_chunks, HELD, CAP, OUT_COLS), bf16),
            dma, dma((K_CHUNKS,)), dma((K_CHUNKS,)), dma((DOWN_SLOTS,)),
            dma((K_CHUNKS, HELD - 1)), dma((K_CHUNKS, HELD - 1)),
            dma((K_CHUNKS, HELD)), dma((K_CHUNKS, HELD)),
            dma((tiles,)), dma((tiles,)), dma((tiles,)), dma((tiles,)),
            dma((out_chunks,)), dma((out_chunks,)),
            dma((out_chunks, HELD - 1)), dma((out_chunks, HELD - 1)),
        ],
        compiler_params=pltpu.CompilerParams(
            collective_id=0, has_side_effects=True, vmem_limit_bytes=64000000
        ),
        cost_estimate=pl.CostEstimate(
            flops=12 * half * depth * hidden, bytes_accessed=6 * depth * hidden, transcendentals=0
        ),
    )(expert_ids.T, gate_int.T, tokens, w_gate, w_up, w_down)


def silu_product(gate_up):
    return (jax.nn.silu(gate_up[:, 0]) * gate_up[:, 1]).astype(jnp.bfloat16)


def expert_rows(received, w_gate, w_up, w_down):
    columns = received.shape[-1]
    leading = received.shape[:-1]
    flattened = received.reshape(-1, columns)
    gate_part = jnp.dot(flattened, w_gate[0], preferred_element_type=jnp.float32)
    up_part = jnp.dot(flattened, w_up[0], preferred_element_type=jnp.float32)
    gate_up = jnp.stack([gate_part, up_part], axis=1)
    summed_half = lax.psum_scatter(gate_up, "tp", scatter_dimension=2, tiled=True)
    hidden = lax.all_gather(silu_product(summed_half), "tp", axis=1, tiled=True)
    partial_value = jnp.dot(hidden, w_down[0], preferred_element_type=jnp.float32).astype(
        jnp.bfloat16
    )
    return partial_value.reshape(leading + (partial_value.shape[-1],))


def send_back(partial_value):
    return lax.all_to_all(partial_value, "ep", split_axis=0, concat_axis=0, tiled=True)


def fits(tokens, w_gate, w_down):
    depth, hidden = w_gate.shape[1:]
    return (
        lax.axis_size("ep") == HELD * MEMBERS
        and lax.axis_size("tp") == 2
        and tokens.shape[0] == HELD * CAP
        and depth % (128 * K_CHUNKS) == 0
        and hidden % 128 == 0
        and w_down.shape[2] % OUT_COLS == 0
    )


def shards(tokens, expert_ids, gate_int, w_gate, w_up, w_down):
    if fits(tokens, w_gate, w_down):
        return fused_shards(tokens, expert_ids, gate_int, w_gate, w_up, w_down)
    row_count = tokens.shape[0]
    experts = lax.broadcasted_iota(jnp.int32, (HELD, 1, 1), 0)
    named = expert_ids[None, :, :] == experts
    weighting = jnp.sum(
        jnp.where(named, gate_int[None, :, :].astype(jnp.float32) / 64.0, jnp.float32(0.0)), axis=2
    )
    chosen = jnp.any(named, axis=2).astype(jnp.int32)
    slot_of = jnp.cumsum(chosen, axis=1) - 1
    slot_ids = lax.broadcasted_iota(jnp.int32, (HELD, CAP, row_count), 1)
    placed = (chosen[:, None, :] == 1) & (slot_of[:, None, :] == slot_ids)
    outgoing = jnp.einsum(
        "ecr,rd->ecd", placed.astype(jnp.bfloat16), tokens, preferred_element_type=jnp.float32
    ).astype(jnp.bfloat16)
    members = lax.axis_size("ep") // HELD
    outgoing = jnp.repeat(outgoing, members, axis=0)
    received = lax.all_to_all(outgoing, "ep", split_axis=0, concat_axis=0, tiled=True)
    returned = send_back(expert_rows(received, w_gate, w_up, w_down))
    columns = returned.shape[-1]
    summed = jnp.sum(returned.reshape(HELD, members, CAP, columns).astype(jnp.float32), axis=1)
    weighted = placed.astype(jnp.float32) * weighting[:, None, :]
    combined = jnp.einsum("ecr,ecd->rd", weighted, summed, precision=lax.Precision.HIGHEST)
    return combined.astype(jnp.bfloat16)


def solution(mesh):
    return jax.shard_map(
        shards,
        mesh=mesh,
        in_specs=(
            P(("rep", "ep"), "tp"),
            P(("rep", "ep"), None),
            P(("rep", "ep"), None),
            P("ep", "tp", None),
            P("ep", "tp", None),
            P("ep", None, "tp"),
        ),
        out_specs=P(("rep", "ep"), "tp"),
        check_vma=False,
    )
```

```python
import functools

import jax
import jax.numpy as jnp
from jax import lax
from jax.experimental import pallas as pl
from jax.experimental.pallas import tpu as pltpu
from jax.sharding import PartitionSpec as P

HELD = 4
CAP = 32
MEMBERS = 2
K_CHUNKS = 3
OUT_COLS = 768
HID_COLS = 768
DOWN_SLOTS = 2


def remote(src, dst, send_sem, recv_sem, axis, index):
    return pltpu.make_async_remote_copy(
        src_ref=src,
        dst_ref=dst,
        send_sem=send_sem,
        recv_sem=recv_sem,
        device_id={axis: index},
        device_id_type=pl.DeviceIdType.MESH,
    )


def fused_kernel(
    ids_ref, gint_ref, tok_hbm, wg_hbm, wu_hbm, wd_hbm, out_ref,
    tok, wg, wu, wd, send, recv, acc_g, acc_u, gu_send, gu_recv, hid,
    part, part_in, own, total, ret,
    tok_sem, wg_sem, wu_sem, wd_sem,
    z_send, z_recv, x_send, x_recv, gu_ss, gu_rs, hid_ss, hid_rs,
    px_send, px_recv, rz_send, rz_recv,
):
    rows, depth = tok.shape
    hidden = wg.shape[1]
    out_cols = wd.shape[2]
    out_chunks = part.shape[0]
    kw = depth // K_CHUNKS
    half = HELD * CAP
    me = lax.axis_index("ep")
    mine = lax.div(me, MEMBERS)
    x = lax.rem(me, MEMBERS)
    t = lax.axis_index("tp")
    x_peer = mine * MEMBERS + 1 - x
    t_peer = 1 - t
    my_row = pl.multiple_of(t * half, half)
    peer_row = pl.multiple_of(t_peer * half, half)
    full_tiles = hidden // HID_COLS
    tail = hidden % HID_COLS

    def z_to(d):
        return lax.rem(mine + d, HELD)

    def z_from(d):
        return lax.rem(mine + HELD - d, HELD)

    def over_tiles(body):
        def step(n, carry):
            body(n, pl.ds(pl.multiple_of(n * HID_COLS, HID_COLS), HID_COLS))
            return carry

        lax.fori_loop(0, full_tiles, step, 0)
        if tail:
            body(full_tiles, pl.ds(full_tiles * HID_COLS, tail))

    tok_copy = pltpu.make_async_copy(tok_hbm, tok, tok_sem)
    tok_copy.start()

    def weight_copies(k):
        band = pl.ds(k * kw, kw)
        return (
            pltpu.make_async_copy(wg_hbm.at[0, band], wg.at[band], wg_sem.at[k]),
            pltpu.make_async_copy(wu_hbm.at[0, band], wu.at[band], wu_sem.at[k]),
        )

    def down_copy(c):
        return pltpu.make_async_copy(
            wd_hbm.at[0, :, pl.ds(c * out_cols, out_cols)],
            wd.at[c % DOWN_SLOTS],
            wd_sem.at[c % DOWN_SLOTS],
        )

    for k in range(K_CHUNKS):
        for copy in weight_copies(k):
            copy.start()
    for c in range(min(DOWN_SLOTS, out_chunks)):
        down_copy(c).start()

    barrier = pltpu.get_barrier_semaphore()
    for d in range(1, HELD):
        pl.semaphore_signal(
            barrier, inc=1, device_id={"ep": z_to(d) * MEMBERS + x},
            device_id_type=pl.DeviceIdType.MESH,
        )
    pl.semaphore_signal(
        barrier, inc=1, device_id={"ep": x_peer}, device_id_type=pl.DeviceIdType.MESH
    )
    pl.semaphore_signal(
        barrier, inc=1, device_id={"tp": t_peer}, device_id_type=pl.DeviceIdType.MESH
    )

    spot = lax.broadcasted_iota(jnp.int32, (half, rows), 0)
    spot_expert = lax.div(spot, CAP)
    spot_slot = lax.rem(spot, CAP).astype(jnp.float32)
    chosen = jnp.zeros((half, rows), jnp.float32)
    weight = jnp.zeros((half, rows), jnp.float32)
    for j in range(ids_ref.shape[0]):
        hit = ids_ref[j : j + 1] == spot_expert
        chosen = chosen + jnp.where(hit, 1.0, 0.0)
        weight = weight + jnp.where(hit, gint_ref[j : j + 1].astype(jnp.float32) / 64.0, 0.0)
    upper = (
        lax.broadcasted_iota(jnp.int32, (rows, rows), 0)
        <= lax.broadcasted_iota(jnp.int32, (rows, rows), 1)
    )
    rank = jnp.dot(
        chosen.astype(jnp.bfloat16),
        jnp.where(upper, 1.0, 0.0).astype(jnp.bfloat16),
        preferred_element_type=jnp.float32,
    )
    placed = jnp.where(rank == spot_slot + 1.0, chosen, 0.0)
    weighted = jnp.transpose(placed * weight).astype(jnp.bfloat16)
    placed = placed.astype(jnp.bfloat16)

    pl.semaphore_wait(barrier, HELD + 1)
    tok_copy.wait()

    def z_copy(k, d):
        return remote(
            send.at[k, z_to(d)], recv.at[k, 0, mine], z_send.at[k, d - 1],
            z_recv.at[k, d - 1], "ep", z_to(d) * MEMBERS + x,
        )

    def x_copy(k, d):
        block = z_from(d)
        return remote(
            recv.at[k, 0, block], recv.at[k, 1, block], x_send.at[k, d],
            x_recv.at[k, d], "ep", x_peer,
        )

    for k in range(K_CHUNKS):
        packed = jnp.dot(
            placed, tok[:, k * kw : (k + 1) * kw], preferred_element_type=jnp.float32
        ).astype(jnp.bfloat16)
        send[k] = packed.reshape(HELD, CAP, kw)
        for d in (2, 1, 3):
            z_copy(k, d).start()
        recv[k, 0, mine] = send[k, mine]
        x_copy(k, 0).start()

    def forward(k):
        for d in (1, 3, 2):
            z_copy(k, d).wait_recv()
            x_copy(k, d).start()

    def project(k):
        for copy in weight_copies(k):
            copy.wait()
        for d in range(HELD):
            x_copy(k, d).wait_recv()
        band = pl.ds(k * kw, kw)

        def tile(n, cols):
            lhs = recv[k].reshape(MEMBERS * half, kw)
            for w, acc in ((wg, acc_g), (wu, acc_u)):
                value = jnp.dot(lhs, w[band, cols], preferred_element_type=jnp.float32)
                if k > 0:
                    value = value + acc[:, cols]
                acc[:, cols] = value
            if k == K_CHUNKS - 1:
                for i, acc in enumerate((acc_g, acc_u)):
                    gu_send[i, :, cols] = acc[pl.ds(peer_row, half), cols].astype(jnp.bfloat16)
                gu_copy(n, cols).start()

        over_tiles(tile)

    def gu_copy(n, cols):
        return remote(
            gu_send.at[:, :, cols], gu_recv.at[:, :, cols], gu_ss.at[n], gu_rs.at[n], "tp", t_peer
        )

    def hid_copy(n, cols):
        span = hid.at[pl.ds(my_row, half), cols]
        return remote(span, span, hid_ss.at[n], hid_rs.at[n], "tp", t_peer)

    forward(0)
    for k in range(1, K_CHUNKS):
        forward(k)
        project(k - 1)
    project(K_CHUNKS - 1)

    def activate(n, cols):
        gu_copy(n, cols).wait_recv()
        gate = acc_g[pl.ds(my_row, half), cols] + gu_recv[0, :, cols].astype(jnp.float32)
        up = acc_u[pl.ds(my_row, half), cols] + gu_recv[1, :, cols].astype(jnp.float32)
        hid[pl.ds(my_row, half), cols] = (jax.nn.silu(gate) * up).astype(jnp.bfloat16)
        hid_copy(n, cols).start()

    over_tiles(activate)
    over_tiles(lambda n, cols: hid_copy(n, cols).wait_recv())

    def part_copy(c):
        return remote(part.at[c], part_in.at[c], px_send.at[c], px_recv.at[c], "ep", x_peer)

    def ret_copy(c, d):
        return remote(
            total.at[c, z_to(d)], ret.at[c, mine], rz_send.at[c, d - 1], rz_recv.at[c, d - 1],
            "ep", z_to(d) * MEMBERS + x,
        )

    for c in range(out_chunks):
        down_copy(c).wait()
        value = jnp.dot(
            hid[...], wd[c % DOWN_SLOTS], preferred_element_type=jnp.float32
        ).astype(jnp.bfloat16)
        part[c] = value[half:]
        part_copy(c).start()
        own[c] = value[:half]
        if c + DOWN_SLOTS < out_chunks:
            down_copy(c + DOWN_SLOTS).start()

    for c in range(out_chunks):
        part_copy(c).wait_recv()
        value = (own[c].astype(jnp.float32) + part_in[c].astype(jnp.float32)).astype(jnp.bfloat16)
        total[c] = value.reshape(HELD, CAP, out_cols)
        for d in (2, 1, 3):
            ret_copy(c, d).start()
        ret[c, mine] = total[c, mine]

    for c in range(out_chunks):
        for d in range(1, HELD):
            ret_copy(c, d).wait_recv()
        out_ref[:, c * out_cols : (c + 1) * out_cols] = jnp.dot(
            weighted, ret[c].reshape(half, out_cols), preferred_element_type=jnp.float32
        ).astype(jnp.bfloat16)

    for k in range(K_CHUNKS):
        for d in range(HELD):
            x_copy(k, d).wait_send()
            if d > 0:
                z_copy(k, d).wait_send()
    over_tiles(lambda n, cols: gu_copy(n, cols).wait_send())
    over_tiles(lambda n, cols: hid_copy(n, cols).wait_send())
    for c in range(out_chunks):
        part_copy(c).wait_send()
        for d in range(1, HELD):
            ret_copy(c, d).wait_send()


def fused_shards(tokens, expert_ids, gate_int, w_gate, w_up, w_down):
    rows, depth = tokens.shape
    hidden = w_gate.shape[2]
    columns = w_down.shape[2]
    out_chunks = columns // OUT_COLS
    half = HELD * CAP
    kw = depth // K_CHUNKS
    tiles = pl.cdiv(hidden, HID_COLS)
    bf16, f32 = jnp.bfloat16, jnp.float32
    dma = pltpu.SemaphoreType.DMA
    return pl.pallas_call(
        fused_kernel,
        out_shape=jax.ShapeDtypeStruct((rows, columns), bf16),
        in_specs=[pl.BlockSpec(memory_space=pltpu.VMEM)] * 2
        + [pl.BlockSpec(memory_space=pl.ANY)] * 4,
        out_specs=pl.BlockSpec(memory_space=pltpu.VMEM),
        scratch_shapes=[
            pltpu.VMEM((rows, depth), bf16),
            pltpu.VMEM((depth, hidden), bf16),
            pltpu.VMEM((depth, hidden), bf16),
            pltpu.VMEM((DOWN_SLOTS, hidden, OUT_COLS), bf16),
            pltpu.VMEM((K_CHUNKS, HELD, CAP, kw), bf16),
            pltpu.VMEM((K_CHUNKS, MEMBERS, HELD, CAP, kw), bf16),
            pltpu.VMEM((MEMBERS * half, hidden), f32),
            pltpu.VMEM((MEMBERS * half, hidden), f32),
            pltpu.VMEM((2, half, hidden), bf16),
            pltpu.VMEM((2, half, hidden), bf16),
            pltpu.VMEM((MEMBERS * half, hidden), bf16),
            pltpu.VMEM((out_chunks, half, OUT_COLS), bf16),
            pltpu.VMEM((out_chunks, half, OUT_COLS), bf16),
            pltpu.VMEM((out_chunks, half, OUT_COLS), bf16),
            pltpu.VMEM((out_chunks, HELD, CAP, OUT_COLS), bf16),
            pltpu.VMEM((out_chunks, HELD, CAP, OUT_COLS), bf16),
            dma, dma((K_CHUNKS,)), dma((K_CHUNKS,)), dma((DOWN_SLOTS,)),
            dma((K_CHUNKS, HELD - 1)), dma((K_CHUNKS, HELD - 1)),
            dma((K_CHUNKS, HELD)), dma((K_CHUNKS, HELD)),
            dma((tiles,)), dma((tiles,)), dma((tiles,)), dma((tiles,)),
            dma((out_chunks,)), dma((out_chunks,)),
            dma((out_chunks, HELD - 1)), dma((out_chunks, HELD - 1)),
        ],
        compiler_params=pltpu.CompilerParams(
            collective_id=0, has_side_effects=True, vmem_limit_bytes=64000000
        ),
        cost_estimate=pl.CostEstimate(
            flops=12 * half * depth * hidden, bytes_accessed=6 * depth * hidden, transcendentals=0
        ),
    )(expert_ids.T, gate_int.T, tokens, w_gate, w_up, w_down)


def silu_product(gate_up):
    return (jax.nn.silu(gate_up[:, 0]) * gate_up[:, 1]).astype(jnp.bfloat16)


def expert_rows(received, w_gate, w_up, w_down):
    columns = received.shape[-1]
    leading = received.shape[:-1]
    flattened = received.reshape(-1, columns)
    gate_part = jnp.dot(flattened, w_gate[0], preferred_element_type=jnp.float32)
    up_part = jnp.dot(flattened, w_up[0], preferred_element_type=jnp.float32)
    gate_up = jnp.stack([gate_part, up_part], axis=1)
    summed_half = lax.psum_scatter(gate_up, "tp", scatter_dimension=2, tiled=True)
    hidden = lax.all_gather(silu_product(summed_half), "tp", axis=1, tiled=True)
    partial_value = jnp.dot(hidden, w_down[0], preferred_element_type=jnp.float32).astype(
        jnp.bfloat16
    )
    return partial_value.reshape(leading + (partial_value.shape[-1],))


def send_back(partial_value):
    return lax.all_to_all(partial_value, "ep", split_axis=0, concat_axis=0, tiled=True)


def fits(tokens, w_gate, w_down):
    depth, hidden = w_gate.shape[1:]
    return (
        lax.axis_size("ep") == HELD * MEMBERS
        and lax.axis_size("tp") == 2
        and tokens.shape[0] == HELD * CAP
        and depth % (128 * K_CHUNKS) == 0
        and hidden % 128 == 0
        and w_down.shape[2] % OUT_COLS == 0
    )


def shards(tokens, expert_ids, gate_int, w_gate, w_up, w_down):
    if fits(tokens, w_gate, w_down):
        return fused_shards(tokens, expert_ids, gate_int, w_gate, w_up, w_down)
    row_count = tokens.shape[0]
    experts = lax.broadcasted_iota(jnp.int32, (HELD, 1, 1), 0)
    named = expert_ids[None, :, :] == experts
    weighting = jnp.sum(
        jnp.where(named, gate_int[None, :, :].astype(jnp.float32) / 64.0, jnp.float32(0.0)), axis=2
    )
    chosen = jnp.any(named, axis=2).astype(jnp.int32)
    slot_of = jnp.cumsum(chosen, axis=1) - 1
    slot_ids = lax.broadcasted_iota(jnp.int32, (HELD, CAP, row_count), 1)
    placed = (chosen[:, None, :] == 1) & (slot_of[:, None, :] == slot_ids)
    outgoing = jnp.einsum(
        "ecr,rd->ecd", placed.astype(jnp.bfloat16), tokens, preferred_element_type=jnp.float32
    ).astype(jnp.bfloat16)
    members = lax.axis_size("ep") // HELD
    outgoing = jnp.repeat(outgoing, members, axis=0)
    received = lax.all_to_all(outgoing, "ep", split_axis=0, concat_axis=0, tiled=True)
    returned = send_back(expert_rows(received, w_gate, w_up, w_down))
    columns = returned.shape[-1]
    summed = jnp.sum(returned.reshape(HELD, members, CAP, columns).astype(jnp.float32), axis=1)
    weighted = placed.astype(jnp.float32) * weighting[:, None, :]
    combined = jnp.einsum("ecr,ecd->rd", weighted, summed, precision=lax.Precision.HIGHEST)
    return combined.astype(jnp.bfloat16)


def solution(mesh):
    return jax.shard_map(
        shards,
        mesh=mesh,
        in_specs=(
            P(("rep", "ep"), "tp"),
            P(("rep", "ep"), None),
            P(("rep", "ep"), None),
            P("ep", "tp", None),
            P("ep", "tp", None),
            P("ep", None, "tp"),
        ),
        out_specs=P(("rep", "ep"), "tp"),
        check_vma=False,
    )
```
